32 devices in a mesh: parts: 2 (over x), expert: 8 (over z, core), cuts: 2 (over y).
Axes of the slice: x: 2, y: 2, z: 4, core: 2. Of those that a mesh axis runs over, the one named last changes fastest.
Arguments:
- tokens: bfloat16 [128, 7168], P(('parts', 'expert', 'cuts')), parts along dimension 0, may hold values from -6 to 6
- route_ids: int32 [128, 8], P(('parts', 'expert', 'cuts')), parts along dimension 0, may hold values from 0 to 15, all different within a row; in each aligned block of 4 rows (0 to 3, 4 to 7, ...) at most 3 rows name the same one
- route_weight: float32 [128, 8], P(('parts', 'expert', 'cuts')), parts along dimension 0, may hold values from 0.05 to 0.5
- gate_weight: bfloat16 [16, 7168, 1024], P('expert', None, 'cuts'), may hold values from -0.0625 to 0.0625
- up_weight: bfloat16 [16, 7168, 1024], P('expert', None, 'cuts'), may hold values from -0.0625 to 0.0625
- down_weight: bfloat16 [16, 1024, 7168], P('expert', 'cuts'), may hold values from -0.1875 to 0.1875
Outputs:
- mixed: bfloat16 [128, 7168], P(('parts', 'expert', 'cuts')), parts along dimension 0
The draws below stay inside these ranges and needn't reach their ends.
There are 2 independent parts, one for each index of `parts`. The reference program is written for one: setup_inputs(seed, part) draws one part's arguments, and reference() takes and returns one part's arrays. A program takes and returns all parts, laid end to end along the dimension named above; an argument that names none is the same for every part. Nothing has to cross between parts.
Inputs may be any that keep to these rules, and one draw needn't show every extreme that they name: `route_ids`: each row names 8 different experts. Among the rows of one device no expert is named more than 3 times, and in every draw some device's rows name some expert exactly 3 times.
All inputs are finite; a program needn't handle non-finite values. Where the reference program divides by a largest or mean magnitude, that divisor is 1e-20 or more.
Results may differ from the reference program's by a relative error of at most 0.02.
Values may be sent and summed in bfloat16 or wider, within the bound.
A program may use at most 128 MiB of HBM per device.

```python
import math
import jax
import jax.numpy as jnp
import numpy as np
from jax import lax

D = 7168
FF = 1024
TOP = 8
BLOCK = 128
ROWS = 4
EXPERTS = 16
ROWS_ALL = 64
CAP = 3
N_EXPERT = 8
N_CUTS = 2


def block_levels(key, extent, split, least, high):
    level = 1.0
    for dim, blocks in split:
        steps = jax.random.uniform(jax.random.fold_in(jax.random.fold_in(key, 6), dim), (blocks,), jnp.float32, least / len(split), high / len(split))
        level = level * jnp.repeat(jnp.exp(steps), extent[dim] // blocks).reshape((-1,) + (1,) * (len(extent) - 1 - dim))
    return level


def shared_out(rng, own, number, rows, count, top, reach, skew):
    ranking = jax.random.permutation(rng, count)
    crowded, usual = shares(count, rows * top, reach, skew, True), shares(count, rows * top, reach, skew, False)
    places = jnp.arange(count)

    def named(lengths, turn):
        used = int((lengths > 0).sum())
        fixed = max(1, used // 4)
        passed = fixed + (places - fixed + turn * (used - fixed)) % max(1, count - fixed)
        return jnp.zeros((count,), jnp.int32).at[ranking[jnp.where(places < fixed, places, passed)]].set(jnp.asarray(lengths, jnp.int32))

    lengths = jnp.where(number % 4 == 0, named(crowded, number // 4), named(usual, number - number // 4 - 1))
    mixed = jax.random.permutation(jax.random.fold_in(own, 3), count)
    donor, sink = mixed[0:count // 2 * 2:2], mixed[1:count // 2 * 2:2]
    slack = jnp.minimum(lengths[donor] - 1, reach - lengths[sink]) // 2
    slack = jnp.where((donor == ranking[0]) | (sink == ranking[0]) | (lengths[sink] == 0), 0, jnp.maximum(slack, 0))
    passed = jax.random.randint(jax.random.fold_in(own, 4), (count // 2,), 0, 1 << 20) % (slack + 1)
    lengths = lengths.at[donor].add(-passed).at[sink].add(passed)
    labels = jnp.searchsorted(jnp.cumsum(lengths), jnp.arange(rows * top), side="right").astype(jnp.int32)
    table = labels.reshape(top, rows).T
    table = table[jax.random.permutation(jax.random.fold_in(own, 1), rows)]
    turn = jax.random.randint(jax.random.fold_in(own, 2), (rows, 1), 0, top)
    return jnp.take_along_axis(table, (jnp.arange(top)[None, :] + turn) % top, axis=1)


def shares(amount, total, bound, skew, full):
    loads = [(1 << 20) // math.isqrt(standing ** skew) + 1 for standing in range(1, amount + 1)]
    largest = bound if full else min(bound, max(-(-total // amount), total * loads[0] // sum(loads)))
    least = 1 if total - largest >= amount - 1 else 0
    counts, rest = [largest] + [least] * (amount - 1), total - largest - least * (amount - 1)
    while rest > 0:
        movable = [i for i in range(1, amount) if counts[i] < largest] or [i for i in range(1, amount) if counts[i] < bound]
        mass, budget = sum([loads[i] for i in movable]), rest
        for i in movable:
            more = min(bound - counts[i], max(1, budget * loads[i] // mass), rest)
            counts[i] = counts[i] + more
            rest = rest - more
    return np.array(counts)


def gaussian(stream_key, shape, width, limit, cuts=(), held_as=jnp.bfloat16):
    gain = block_levels(stream_key, shape, cuts, -0.22, 0.18) if cuts else 1.0
    drawn = jax.random.normal(stream_key, shape, jnp.float32) * width * gain
    return jnp.minimum(jnp.maximum(drawn, -limit), limit).astype(held_as)


def setup_inputs(seed: int = 0, part: int = 0) -> dict:
    keys = jax.random.split(jax.random.key(seed), 7)
    part_splits = jax.random.split(jax.random.fold_in(keys[6], part), 7)
    tokens = gaussian(part_splits[0], (ROWS_ALL, D), 1.0, 6.0, ((0, 16),))
    route_ids_keys = jax.random.split(jax.random.fold_in(part_splits[1], 1), ROWS_ALL // ROWS)
    route_ids_turns = jax.random.permutation(jax.random.fold_in(part_splits[1], 3), ROWS_ALL // ROWS)
    route_ids = jax.vmap(lambda own, number: shared_out(jax.random.fold_in(part_splits[1], 2), own, number, ROWS, EXPERTS, TOP, CAP, 2))(route_ids_keys, route_ids_turns).reshape((ROWS_ALL, TOP))
    route_weight = jnp.clip(jnp.exp(math.log(0.5) - 2.3025851 * jax.random.uniform(part_splits[2], (ROWS_ALL, TOP), jnp.float32) ** block_levels(part_splits[2], (ROWS_ALL, TOP), ((0, 16),), -0.2, 0.2)), 0.05, 0.5)
    gate_weight = gaussian(keys[3], (EXPERTS, D, FF), D ** -0.5, 0.0625, ((0, 8), (2, 2)))
    up_weight = gaussian(keys[4], (EXPERTS, D, FF), D ** -0.5, 0.0625, ((0, 8), (2, 2)))
    down_weight = gaussian(keys[5], (EXPERTS, FF, D), FF ** -0.5, 0.1875, ((0, 8), (1, 2)))
    return {"tokens": tokens, "route_ids": route_ids, "route_weight": route_weight, "gate_weight": gate_weight, "up_weight": up_weight, "down_weight": down_weight}


eps = 1e-06
levels = 127.0

def hadamard(block_size):
    bit_count = block_size.bit_length() - 1
    row_bits = lax.broadcasted_iota(jnp.int32, (block_size, block_size), 0)
    col_bits = lax.broadcasted_iota(jnp.int32, (block_size, block_size), 1)
    shared_bits = jnp.bitwise_and(row_bits, col_bits)
    parity_sum = jnp.zeros((block_size, block_size), jnp.int32)
    for shift_step in range(bit_count):
        parity_sum = parity_sum + jnp.bitwise_and(jnp.right_shift(shared_bits, shift_step), 1)
    return (1 - 2 * (parity_sum % 2)).astype(jnp.bfloat16)

def reference(tokens, route_ids, route_weight, gate_weight, up_weight, down_weight):
    devices = N_EXPERT * N_CUTS
    blocks = D // BLOCK
    sign_table = hadamard(BLOCK)
    rotated = jnp.dot(tokens.reshape(ROWS_ALL * blocks, BLOCK), sign_table, preferred_element_type=jnp.float32) * (1.0 / math.sqrt(BLOCK))
    largest = lax.optimization_barrier(jnp.max(jnp.abs(rotated), axis=1)) + eps
    quantized = jnp.clip(jnp.floor(rotated / largest[:, None] * levels + 0.5), -levels, levels).astype(jnp.bfloat16)
    quantized = lax.optimization_barrier(quantized)
    restored = (quantized.astype(jnp.float32) * largest[:, None] / levels).astype(jnp.bfloat16).reshape(ROWS_ALL, D)
    ids = route_ids.reshape(devices, ROWS * TOP)
    expert_hot = (ids[:, :, None] == jnp.arange(EXPERTS, dtype=jnp.int32)[None, None, :]).astype(jnp.int32)
    earlier = jnp.cumsum(expert_hot, axis=1) - expert_hot
    position = lax.optimization_barrier(jnp.sum(earlier * expert_hot, axis=2)).astype(jnp.int32)
    slot_index = (ids * CAP + position).astype(jnp.int32)
    device_index = jnp.broadcast_to(jnp.arange(devices, dtype=jnp.int32)[:, None], (devices, ROWS * TOP))
    row_global = (device_index * ROWS + jnp.arange(ROWS * TOP, dtype=jnp.int32)[None, :] // TOP).astype(jnp.int32)
    row_table = jnp.zeros((devices, EXPERTS * CAP), jnp.int32).at[device_index, slot_index].set(row_global + 1)
    weight_table = jnp.zeros((devices, EXPERTS * CAP), jnp.float32).at[device_index, slot_index].set(route_weight.reshape(devices, ROWS * TOP))
    row_table = row_table.reshape(devices, EXPERTS, CAP).transpose(1, 0, 2).reshape(EXPERTS, devices * CAP)
    weight_table = weight_table.reshape(devices, EXPERTS, CAP).transpose(1, 0, 2).reshape(EXPERTS, devices * CAP)

    def one_expert(total, inputs):
        row_index, slot_weight, gate_one, up_one, down_one = inputs
        picked = jnp.maximum(row_index - 1, 0).astype(jnp.int32)
        rows_in = restored[picked].astype(jnp.float32)
        gate_value = jnp.dot(rows_in, gate_one.astype(jnp.float32), precision=lax.Precision.HIGHEST)
        upward = jnp.dot(rows_in, up_one.astype(jnp.float32), precision=lax.Precision.HIGHEST)
        hidden = (jax.nn.silu(gate_value) * upward).astype(jnp.bfloat16)
        group = FF // N_CUTS
        pieces = jnp.einsum('scf,cfd->scd', hidden.reshape(-1, N_CUTS, group).astype(jnp.float32), down_one.reshape(N_CUTS, group, D).astype(jnp.float32), precision=lax.Precision.HIGHEST)
        summed = lax.optimization_barrier(jnp.sum(pieces.astype(jnp.bfloat16).astype(jnp.float32), axis=1))
        total = total.at[picked].add(slot_weight[:, None] * summed)
        return (total, None)
    start = jnp.zeros((ROWS_ALL, D), jnp.float32)
    total, unused = lax.scan(one_expert, start, (row_table, weight_table, gate_weight, up_weight, down_weight))
    return total.astype(jnp.bfloat16)
```

```python
import functools
import math

import jax
import jax.numpy as jnp
from jax import lax
from jax.experimental import pallas as pl
from jax.experimental.pallas import tpu as pltpu
from jax.sharding import PartitionSpec as P

BLOCK = 128
eps = 1e-06
levels = 127.0
CORES = 2
QUARTERS = 4
TILE = 16
GROUP = 16
CHUNKS = 2
MESH = pl.DeviceIdType.MESH


def hadamard():
    row_bits = lax.broadcasted_iota(jnp.int32, (BLOCK, BLOCK), 0)
    col_bits = lax.broadcasted_iota(jnp.int32, (BLOCK, BLOCK), 1)
    shared = jnp.bitwise_and(row_bits, col_bits)
    for shift in (4, 2, 1):
        shared = jnp.bitwise_xor(shared, jnp.right_shift(shared, shift))
    return (1 - 2 * jnp.bitwise_and(shared, 1)).astype(jnp.float32).astype(jnp.bfloat16)


def permutation(rows, transposed):
    side = GROUP * TILE
    a = lax.broadcasted_iota(jnp.int32, (side, side), 1 if transposed else 0)
    b = lax.broadcasted_iota(jnp.int32, (side, side), 0 if transposed else 1)
    per = GROUP * rows
    quarter, inner = a // per, a % per
    source = (inner // rows) * TILE + quarter * rows + inner % rows
    return jnp.where(source == b, 1.0, 0.0).astype(jnp.bfloat16)


def kernel(
    n_z,
    n_y,
    tokens,
    ids,
    weights,
    gate_hbm,
    up_hbm,
    down_hbm,
    out,
    gate,
    up,
    down,
    gathered,
    stage,
    acc,
    hid,
    wide,
    y_buf,
    r_core,
    s_buf,
    r_y,
    t_buf,
    r_z,
    final,
    g_sem,
    u_sem,
    d_sem,
    az_send,
    az_recv,
    ay_send,
    ay_recv,
    ac_send,
    ac_recv,
    rc_send,
    rc_recv,
    ry_send,
    ry_recv,
    rz_send,
    rz_recv,
):
    rows, features = tokens.shape
    experts = gate.shape[0]
    units = gate.shape[2]
    width = features // QUARTERS
    chunk = width // CHUNKS
    plane = n_y * n_z
    blocks = CORES * plane
    groups = blocks // GROUP
    expert = lax.axis_index("expert")
    y = lax.axis_index("cuts")
    z, c = expert // CORES, expert % CORES
    far = 1 - c

    def peer(z_at, c_at, y_at):
        return {"expert": z_at * CORES + c_at, "cuts": y_at}

    def block(c_at, y_at, z_at):
        return (c_at * n_y + y_at) * n_z + z_at

    def z_next(step):
        return lax.rem(z + step, n_z)

    def y_next(step):
        return lax.rem(y + step, n_y)

    def z_prev(step):
        return lax.rem(z + n_z - step, n_z)

    def y_prev(step):
        return lax.rem(y + n_y - step, n_y)

    gate_in, up_in, down_in = [], [], []
    for q in range(QUARTERS):
        span = pl.ds(q * width, width)
        gate_in.append(
            pltpu.make_async_copy(gate_hbm.at[:, span, :], gate.at[:, span, :], g_sem.at[q])
        )
        up_in.append(pltpu.make_async_copy(up_hbm.at[:, span, :], up.at[:, span, :], u_sem.at[q]))
        gate_in[q].start()
        up_in[q].start()
    for j in range(CHUNKS):
        for q in range(QUARTERS):
            span = pl.ds(q * width + j * chunk, chunk)
            down_in.append(
                pltpu.make_async_copy(
                    down_hbm.at[:, :, span], down.at[:, :, span], d_sem.at[j * QUARTERS + q]
                )
            )
            down_in[-1].start()

    barrier = pltpu.get_barrier_semaphore()
    for step in range(1, n_z):
        pl.semaphore_signal(
            barrier, inc=1, device_id=peer(z_next(step), c, y), device_id_type=MESH
        )
    for step in range(1, n_y):
        pl.semaphore_signal(
            barrier, inc=1, device_id=peer(z, c, y_next(step)), device_id_type=MESH
        )
    pl.semaphore_signal(barrier, inc=1, device_id=peer(z, far, y), device_id_type=MESH)

    mine = block(c, y, z)
    for q in range(QUARTERS):
        stage[q * rows : (q + 1) * rows, :width] = tokens[:, q * width : (q + 1) * width].astype(
            jnp.float32
        )
    pieces = width // BLOCK
    stacked = jnp.concatenate(
        [stage[:, b * BLOCK : (b + 1) * BLOCK].astype(jnp.bfloat16) for b in range(pieces)], axis=0
    )
    rotated = jnp.dot(stacked, hadamard(), preferred_element_type=jnp.float32) * (
        1.0 / math.sqrt(BLOCK)
    )
    largest = jnp.max(jnp.abs(rotated), axis=1, keepdims=True) + eps
    quantized = jnp.clip(jnp.floor(rotated / largest * levels + 0.5), -levels, levels)
    restored = (quantized * largest / levels).astype(jnp.bfloat16)
    for b in range(pieces):
        gathered[mine, :, b * BLOCK : (b + 1) * BLOCK] = restored[b * TILE : (b + 1) * TILE, :]
    lane = lax.broadcasted_iota(jnp.int32, (rows, BLOCK), 1)
    dense = jnp.zeros((rows, BLOCK), jnp.float32)
    for k in range(ids.shape[1]):
        dense = dense + jnp.where(ids[:, k : k + 1] == lane, weights[:, k : k + 1], 0.0)
    stage[:, width:] = jnp.zeros((TILE, BLOCK), jnp.float32)
    for q in range(3):
        term = dense.astype(jnp.bfloat16).astype(jnp.float32)
        stage[q * rows : (q + 1) * rows, width:] = term
        dense = dense - term
    gathered[mine, :, width:] = stage[:, width:].astype(jnp.bfloat16)

    pl.semaphore_wait(barrier, n_z + n_y - 1)

    sent = []

    def push(src, dst, send_sem, recv_sem, device):
        copy = pltpu.make_async_remote_copy(
            src_ref=src,
            dst_ref=dst,
            send_sem=send_sem,
            recv_sem=recv_sem,
            device_id=device,
            device_id_type=MESH,
        )
        copy.start()
        sent.append(copy)

    def arrived(dst, send_sem, recv_sem, device):
        pltpu.make_async_remote_copy(
            src_ref=dst,
            dst_ref=dst,
            send_sem=send_sem,
            recv_sem=recv_sem,
            device_id=device,
            device_id_type=MESH,
        ).wait_recv()

    def to_y(z_step, slot):
        for step in range(1, n_y):
            push(
                gathered.at[slot],
                gathered.at[slot],
                ay_send.at[step, z_step],
                ay_recv.at[step, z_step],
                peer(z, c, y_next(step)),
            )

    def to_core(y_step, z_step, slot):
        push(
            gathered.at[slot],
            gathered.at[slot],
            ac_send.at[y_step, z_step],
            ac_recv.at[y_step, z_step],
            peer(z, far, y),
        )

    for step in range(n_z - 1, 0, -1):
        push(
            gathered.at[mine],
            gathered.at[mine],
            az_send.at[step],
            az_recv.at[step],
            peer(z_next(step), c, y),
        )
    to_y(0, mine)
    to_core(0, 0, mine)
    for z_step in range(1, n_z):
        slot = block(c, y, z_prev(z_step))
        arrived(
            gathered.at[slot], az_send.at[z_step], az_recv.at[z_step], peer(z_next(z_step), c, y)
        )
        to_y(z_step, slot)
        to_core(0, z_step, slot)
    for z_step in range(n_z):
        for y_step in range(1, n_y):
            slot = block(c, y_prev(y_step), z_prev(z_step))
            arrived(
                gathered.at[slot],
                ay_send.at[y_step, z_step],
                ay_recv.at[y_step, z_step],
                peer(z, c, y_next(y_step)),
            )
            to_core(y_step, z_step, slot)
    for z_step in range(n_z):
        for y_step in range(n_y):
            slot = block(far, y_prev(y_step), z_prev(z_step))
            arrived(
                gathered.at[slot],
                ac_send.at[y_step, z_step],
                ac_recv.at[y_step, z_step],
                peer(z, far, y),
            )

    order = permutation(rows, False)
    per = GROUP * rows
    route = []
    for g in range(groups):
        flat = gathered[g * GROUP : (g + 1) * GROUP].reshape(GROUP * TILE, width + BLOCK)
        ordered = jnp.dot(order, flat, preferred_element_type=jnp.float32)
        wide[g] = ordered[:, :width].astype(jnp.bfloat16)
        terms = ordered[:, width:]
        route.append(terms[:per] + terms[per : 2 * per] + terms[2 * per : 3 * per])
    for q in range(QUARTERS):
        span = slice(q * width, (q + 1) * width)
        gate_in[q].wait()
        for g in range(groups):
            x = wide[g, q * per : (q + 1) * per, :]
            for e in range(experts):
                part = jnp.dot(x, gate[e, span, :], preferred_element_type=jnp.float32)
                acc[g, 0, e] = part if q == 0 else acc[g, 0, e] + part
        up_in[q].wait()
        for g in range(groups):
            x = wide[g, q * per : (q + 1) * per, :]
            for e in range(experts):
                part = jnp.dot(x, up[e, span, :], preferred_element_type=jnp.float32)
                acc[g, 1, e] = part if q == 0 else acc[g, 1, e] + part
    lanes = lax.broadcasted_iota(jnp.int32, (per, BLOCK), 1)
    scale = []
    for g in range(groups):
        for e in range(experts):
            v = acc[g, 0, e]
            hid[g, e] = (v / (1.0 + jnp.exp(-v)) * acc[g, 1, e]).astype(jnp.bfloat16)
            hit = lanes == expert * experts + e
            scale.append(jnp.sum(jnp.where(hit, route[g], 0.0), axis=1, keepdims=True))

    back = permutation(rows, True)

    def produce(j):
        for q in range(QUARTERS):
            down_in[j * QUARTERS + q].wait()
        for g in range(groups):
            parts = []
            for q in range(QUARTERS):
                span = slice(q * width + j * chunk, q * width + (j + 1) * chunk)
                total = None
                for e in range(experts):
                    part = scale[g * experts + e] * jnp.dot(
                        hid[g, e], down[e, :, span], preferred_element_type=jnp.float32
                    )
                    total = part if total is None else total + part
                parts.append(total.astype(jnp.bfloat16))
            tiled = jnp.dot(
                back, jnp.concatenate(parts, axis=0), preferred_element_type=jnp.float32
            )
            y_buf[j, g * GROUP : (g + 1) * GROUP] = tiled.astype(jnp.bfloat16).reshape(
                GROUP, TILE, chunk
            )
        push(
            y_buf.at[j, pl.ds(far * plane, plane)],
            r_core.at[j],
            rc_send.at[j],
            rc_recv.at[j],
            peer(z, far, y),
        )

    def pair(j, y_at):
        own = y_buf[j, pl.ds(block(c, y_at, 0), n_z)].astype(jnp.float32)
        return own + r_core[j, pl.ds(y_at * n_z, n_z)].astype(jnp.float32)

    def over_y(j):
        arrived(r_core.at[j], rc_send.at[j], rc_recv.at[j], peer(z, far, y))
        for step in range(1, n_y):
            s_buf[j, step - 1] = pair(j, y_next(step)).astype(jnp.bfloat16)
            push(
                s_buf.at[j, step - 1],
                r_y.at[j, step - 1],
                ry_send.at[j, step],
                ry_recv.at[j, step],
                peer(z, c, y_next(step)),
            )

    def over_z(j):
        total = pair(j, y)
        for step in range(1, n_y):
            arrived(
                r_y.at[j, step - 1],
                ry_send.at[j, step],
                ry_recv.at[j, step],
                peer(z, c, y_next(step)),
            )
            total = total + r_y[j, step - 1].astype(jnp.float32)
        t_buf[j] = total.astype(jnp.bfloat16)
        for step in range(n_z - 1, 0, -1):
            push(
                t_buf.at[j, z_next(step)],
                r_z.at[j, step - 1],
                rz_send.at[j, step],
                rz_recv.at[j, step],
                peer(z_next(step), c, y),
            )

    def finish(j):
        total = t_buf[j, z].astype(jnp.float32)
        for step in range(1, n_z):
            arrived(
                r_z.at[j, step - 1],
                rz_send.at[j, step],
                rz_recv.at[j, step],
                peer(z_next(step), c, y),
            )
            total = total + r_z[j, step - 1].astype(jnp.float32)
        final[...] = total
        for q in range(QUARTERS):
            span = slice(q * width + j * chunk, q * width + (j + 1) * chunk)
            out[:, span] = final[q * rows : (q + 1) * rows, :].astype(out.dtype)

    for t in range(CHUNKS + 3):
        for late, stage_of in enumerate((produce, over_y, over_z, finish)):
            if 0 <= t - late < CHUNKS:
                stage_of(t - late)
    for copy in sent:
        copy.wait_send()


def body(tokens, route_ids, route_weight, gate_weight, up_weight, down_weight):
    rows, features = tokens.shape
    n_z = lax.axis_size("expert") // CORES
    n_y = lax.axis_size("cuts")
    experts, _, units = gate_weight.shape
    width = features // QUARTERS
    chunk = width // CHUNKS
    plane = n_z * n_y
    blocks = CORES * plane
    groups = blocks // GROUP
    bf16, f32 = jnp.bfloat16, jnp.float32
    dma = pltpu.SemaphoreType.DMA
    vmem = pl.BlockSpec(memory_space=pltpu.VMEM)
    hbm = pl.BlockSpec(memory_space=pl.ANY)
    return pl.pallas_call(
        functools.partial(kernel, n_z, n_y),
        out_shape=jax.ShapeDtypeStruct((rows, features), bf16),
        in_specs=[vmem, vmem, vmem, hbm, hbm, hbm],
        out_specs=vmem,
        scratch_shapes=[
            pltpu.VMEM(gate_weight.shape, bf16),
            pltpu.VMEM(up_weight.shape, bf16),
            pltpu.VMEM(down_weight.shape, bf16),
            pltpu.VMEM((blocks, TILE, width + BLOCK), bf16),
            pltpu.VMEM((TILE, width + BLOCK), f32),
            pltpu.VMEM((groups, 2, experts, GROUP * rows, units), f32),
            pltpu.VMEM((groups, experts, GROUP * rows, units), bf16),
            pltpu.VMEM((groups, GROUP * TILE, width), bf16),
            pltpu.VMEM((CHUNKS, blocks, TILE, chunk), bf16),
            pltpu.VMEM((CHUNKS, plane, TILE, chunk), bf16),
            pltpu.VMEM((CHUNKS, n_y - 1, n_z, TILE, chunk), bf16),
            pltpu.VMEM((CHUNKS, n_y - 1, n_z, TILE, chunk), bf16),
            pltpu.VMEM((CHUNKS, n_z, TILE, chunk), bf16),
            pltpu.VMEM((CHUNKS, n_z - 1, TILE, chunk), bf16),
            pltpu.VMEM((TILE, chunk), f32),
            dma((QUARTERS,)),
            dma((QUARTERS,)),
            dma((CHUNKS * QUARTERS,)),
            dma((n_z,)),
            dma((n_z,)),
            dma((n_y, n_z)),
            dma((n_y, n_z)),
            dma((n_y, n_z)),
            dma((n_y, n_z)),
            dma((CHUNKS,)),
            dma((CHUNKS,)),
            dma((CHUNKS, n_y)),
            dma((CHUNKS, n_y)),
            dma((CHUNKS, n_z)),
            dma((CHUNKS, n_z)),
        ],
        compiler_params=pltpu.CompilerParams(
            collective_id=0, has_side_effects=True, vmem_limit_bytes=60 * 1024 * 1024
        ),
    )(tokens, route_ids, route_weight, gate_weight, up_weight, down_weight)


def solution(mesh):
    in_specs = (
        P(("parts", "expert", "cuts"), None),
        P(("parts", "expert", "cuts"), None),
        P(("parts", "expert", "cuts"), None),
        P("expert", None, "cuts"),
        P("expert", None, "cuts"),
        P("expert", "cuts", None),
    )
    out_specs = P(("parts", "expert", "cuts"), None)
    return jax.shard_map(body, mesh=mesh, in_specs=in_specs, out_specs=out_specs, check_vma=False)
```

```python
import functools
import math

import jax
import jax.numpy as jnp
from jax import lax
from jax.experimental import pallas as pl
from jax.experimental.pallas import tpu as pltpu
from jax.sharding import PartitionSpec as P

BLOCK = 128
eps = 1e-06
levels = 127.0
CORES = 2
QUARTERS = 4
TILE = 16
GROUP = 16
CHUNKS = 7
LAG = 3
MESH = pl.DeviceIdType.MESH


def hadamard():
    row_bits = lax.broadcasted_iota(jnp.int32, (BLOCK, BLOCK), 0)
    col_bits = lax.broadcasted_iota(jnp.int32, (BLOCK, BLOCK), 1)
    shared = jnp.bitwise_and(row_bits, col_bits)
    for shift in (4, 2, 1):
        shared = jnp.bitwise_xor(shared, jnp.right_shift(shared, shift))
    return (1 - 2 * jnp.bitwise_and(shared, 1)).astype(jnp.float32).astype(jnp.bfloat16)


def permutation(rows, transposed):
    side = GROUP * TILE
    a = lax.broadcasted_iota(jnp.int32, (side, side), 1 if transposed else 0)
    b = lax.broadcasted_iota(jnp.int32, (side, side), 0 if transposed else 1)
    per = GROUP * rows
    quarter, inner = a // per, a % per
    source = (inner // rows) * TILE + quarter * rows + inner % rows
    return jnp.where(source == b, 1.0, 0.0).astype(jnp.bfloat16)


def kernel(
    n_z,
    n_y,
    tokens,
    ids,
    weights,
    gate_hbm,
    up_hbm,
    down_hbm,
    out,
    gate,
    up,
    down,
    gathered,
    stage,
    acc,
    hid,
    wide,
    y_buf,
    r_core,
    s_buf,
    r_y,
    t_buf,
    r_z,
    final,
    g_sem,
    u_sem,
    d_sem,
    az_send,
    az_recv,
    ay_send,
    ay_recv,
    ac_send,
    ac_recv,
    rc_send,
    rc_recv,
    ry_send,
    ry_recv,
    rz_send,
    rz_recv,
):
    rows, features = tokens.shape
    experts = gate.shape[0]
    units = gate.shape[2]
    width = features // QUARTERS
    chunk = width // CHUNKS
    plane = n_y * n_z
    blocks = CORES * plane
    groups = blocks // GROUP
    expert = lax.axis_index("expert")
    y = lax.axis_index("cuts")
    z, c = expert // CORES, expert % CORES
    far = 1 - c
    cut = (width // 256 + 1) // 2 * 256
    spans = ((0, cut), (cut, width + BLOCK))

    def peer(z_at, c_at, y_at):
        return {"expert": z_at * CORES + c_at, "cuts": y_at}

    def block(c_at, y_at, z_at):
        return (c_at * n_y + y_at) * n_z + z_at

    def z_next(step):
        return lax.rem(z + step, n_z)

    def y_next(step):
        return lax.rem(y + step, n_y)

    def z_prev(step):
        return lax.rem(z + n_z - step, n_z)

    def y_prev(step):
        return lax.rem(y + n_y - step, n_y)

    gate_in, up_in, down_in = [], [], []
    for h in range(2):
        low, high = spans[h][0], min(spans[h][1], width)
        for q in range(QUARTERS):
            span = pl.ds(q * width + low, high - low)
            at = h * QUARTERS + q
            gate_in.append(
                pltpu.make_async_copy(gate_hbm.at[:, span, :], gate.at[:, span, :], g_sem.at[at])
            )
            up_in.append(
                pltpu.make_async_copy(up_hbm.at[:, span, :], up.at[:, span, :], u_sem.at[at])
            )
            gate_in[at].start()
            up_in[at].start()
    for e in range(experts):
        down_in.append(pltpu.make_async_copy(down_hbm.at[e], down.at[e], d_sem.at[e]))
        down_in[e].start()

    barrier = pltpu.get_barrier_semaphore()
    for step in range(1, n_z):
        pl.semaphore_signal(
            barrier, inc=1, device_id=peer(z_next(step), c, y), device_id_type=MESH
        )
    for step in range(1, n_y):
        pl.semaphore_signal(
            barrier, inc=1, device_id=peer(z, c, y_next(step)), device_id_type=MESH
        )
    pl.semaphore_signal(barrier, inc=1, device_id=peer(z, far, y), device_id_type=MESH)

    mine = block(c, y, z)
    for q in range(QUARTERS):
        stage[q * rows : (q + 1) * rows, :width] = tokens[:, q * width : (q + 1) * width].astype(
            jnp.float32
        )
    pieces = width // BLOCK
    stacked = jnp.concatenate(
        [stage[:, b * BLOCK : (b + 1) * BLOCK].astype(jnp.bfloat16) for b in range(pieces)], axis=0
    )
    rotated = jnp.dot(stacked, hadamard(), preferred_element_type=jnp.float32) * (
        1.0 / math.sqrt(BLOCK)
    )
    largest = jnp.max(jnp.abs(rotated), axis=1, keepdims=True) + eps
    quantized = jnp.clip(jnp.floor(rotated / largest * levels + 0.5), -levels, levels)
    restored = (quantized * largest / levels).astype(jnp.bfloat16)
    for b in range(pieces):
        gathered[mine, :, b * BLOCK : (b + 1) * BLOCK] = restored[b * TILE : (b + 1) * TILE, :]
    lane = lax.broadcasted_iota(jnp.int32, (rows, BLOCK), 1)
    dense = jnp.zeros((rows, BLOCK), jnp.float32)
    for k in range(ids.shape[1]):
        dense = dense + jnp.where(ids[:, k : k + 1] == lane, weights[:, k : k + 1], 0.0)
    stage[:, width:] = jnp.zeros((TILE, BLOCK), jnp.float32)
    for q in range(3):
        term = dense.astype(jnp.bfloat16).astype(jnp.float32)
        stage[q * rows : (q + 1) * rows, width:] = term
        dense = dense - term
    gathered[mine, :, width:] = stage[:, width:].astype(jnp.bfloat16)

    pl.semaphore_wait(barrier, n_z + n_y - 1)

    sent = []

    def push(src, dst, send_sem, recv_sem, device):
        copy = pltpu.make_async_remote_copy(
            src_ref=src,
            dst_ref=dst,
            send_sem=send_sem,
            recv_sem=recv_sem,
            device_id=device,
            device_id_type=MESH,
        )
        copy.start()
        sent.append(copy)

    def arrived(dst, send_sem, recv_sem, device):
        pltpu.make_async_remote_copy(
            src_ref=dst,
            dst_ref=dst,
            send_sem=send_sem,
            recv_sem=recv_sem,
            device_id=device,
            device_id_type=MESH,
        ).wait_recv()

    def half(h, slot):
        return gathered.at[slot, :, pl.ds(spans[h][0], spans[h][1] - spans[h][0])]

    def to_y(h, z_step, slot):
        for step in range(1, n_y):
            push(
                half(h, slot),
                half(h, slot),
                ay_send.at[h, step, z_step],
                ay_recv.at[h, step, z_step],
                peer(z, c, y_next(step)),
            )

    def to_core(h, y_step, z_step, slot):
        push(
            half(h, slot),
            half(h, slot),
            ac_send.at[h, y_step, z_step],
            ac_recv.at[h, y_step, z_step],
            peer(z, far, y),
        )

    def begin(h):
        for step in range(1, n_z):
            push(
                half(h, mine),
                half(h, mine),
                az_send.at[h, step],
                az_recv.at[h, step],
                peer(z_next(step), c, y),
            )
        to_y(h, 0, mine)
        to_core(h, 0, 0, mine)

    def from_z(h, z_step):
        slot = block(c, y, z_prev(z_step))
        arrived(
            half(h, slot),
            az_send.at[h, z_step],
            az_recv.at[h, z_step],
            peer(z_next(z_step), c, y),
        )
        to_y(h, z_step, slot)
        to_core(h, 0, z_step, slot)

    def from_y(h, z_step, y_step):
        slot = block(c, y_prev(y_step), z_prev(z_step))
        arrived(
            half(h, slot),
            ay_send.at[h, y_step, z_step],
            ay_recv.at[h, y_step, z_step],
            peer(z, c, y_next(y_step)),
        )
        to_core(h, y_step, z_step, slot)

    def events(h):
        steps = [functools.partial(from_z, h, z_step) for z_step in range(1, n_z)]
        return steps + [
            functools.partial(from_y, h, z_step, y_step)
            for z_step in range(n_z)
            for y_step in range(1, n_y)
        ]

    def from_core(h):
        for z_step in range(n_z):
            for y_step in range(n_y):
                slot = block(far, y_prev(y_step), z_prev(z_step))
                arrived(
                    half(h, slot),
                    ac_send.at[h, y_step, z_step],
                    ac_recv.at[h, y_step, z_step],
                    peer(z, far, y),
                )

    begin(0)
    begin(1)
    first, second = events(0), events(1)
    for event in first[: n_z - 1] + second[: n_z - 1] + first[n_z - 1 :]:
        event()
    pending = second[n_z - 1 :]
    each = -(-len(pending) // (2 * QUARTERS))

    order = permutation(rows, False)
    per = GROUP * rows
    route = []
    for h in range(2):
        for event in pending if h else []:
            event()
        from_core(h)
        low, high = spans[h][0], min(spans[h][1], width)
        for g in range(groups):
            flat = gathered[g * GROUP : (g + 1) * GROUP, :, low : spans[h][1]]
            flat = flat.reshape(GROUP * TILE, spans[h][1] - low)
            ordered = jnp.dot(order, flat, preferred_element_type=jnp.float32)
            wide[g, :, low:high] = ordered[:, : high - low].astype(jnp.bfloat16)
            if h:
                terms = ordered[:, high - low :]
                route.append(terms[:per] + terms[per : 2 * per] + terms[2 * per : 3 * per])
        for q in range(QUARTERS):
            span = slice(q * width + low, q * width + high)
            for side, (held, coming) in enumerate(((gate, gate_in), (up, up_in))):
                coming[h * QUARTERS + q].wait()
                for g in range(groups):
                    x = wide[g, q * per : (q + 1) * per, low:high]
                    for e in range(experts):
                        part = jnp.dot(x, held[e, span, :], preferred_element_type=jnp.float32)
                        acc[g, side, e] = part if h + q == 0 else acc[g, side, e] + part
                if h == 0:
                    for event in pending[:each]:
                        event()
                    pending = pending[each:]
    lanes = lax.broadcasted_iota(jnp.int32, (per, BLOCK), 1)
    scale = []
    for g in range(groups):
        for e in range(experts):
            v = acc[g, 0, e]
            hid[g, e] = (v / (1.0 + jnp.exp(-v)) * acc[g, 1, e]).astype(jnp.bfloat16)
            hit = lanes == expert * experts + e
            scale.append(jnp.sum(jnp.where(hit, route[g], 0.0), axis=1, keepdims=True))

    back = permutation(rows, True)
    for e in range(experts):
        down_in[e].wait()

    def produce(j):
        for g in range(groups):
            parts = []
            for q in range(QUARTERS):
                span = slice(q * width + j * chunk, q * width + (j + 1) * chunk)
                total = None
                for e in range(experts):
                    part = scale[g * experts + e] * jnp.dot(
                        hid[g, e], down[e, :, span], preferred_element_type=jnp.float32
                    )
                    total = part if total is None else total + part
                parts.append(total.astype(jnp.bfloat16))
            tiled = jnp.dot(
                back, jnp.concatenate(parts, axis=0), preferred_element_type=jnp.float32
            )
            y_buf[j, g * GROUP : (g + 1) * GROUP] = tiled.astype(jnp.bfloat16).reshape(
                GROUP, TILE, chunk
            )
        push(
            y_buf.at[j, pl.ds(far * plane, plane)],
            r_core.at[j],
            rc_send.at[j],
            rc_recv.at[j],
            peer(z, far, y),
        )

    def pair(j, y_at):
        own = y_buf[j, pl.ds(block(c, y_at, 0), n_z)].astype(jnp.float32)
        return own + r_core[j, pl.ds(y_at * n_z, n_z)].astype(jnp.float32)

    def over_y(j):
        arrived(r_core.at[j], rc_send.at[j], rc_recv.at[j], peer(z, far, y))
        for step in range(1, n_y):
            s_buf[j, step - 1] = pair(j, y_next(step)).astype(jnp.bfloat16)
            push(
                s_buf.at[j, step - 1],
                r_y.at[j, step - 1],
                ry_send.at[j, step],
                ry_recv.at[j, step],
                peer(z, c, y_next(step)),
            )

    def over_z(j):
        total = pair(j, y)
        for step in range(1, n_y):
            arrived(
                r_y.at[j, step - 1],
                ry_send.at[j, step],
                ry_recv.at[j, step],
                peer(z, c, y_next(step)),
            )
            total = total + r_y[j, step - 1].astype(jnp.float32)
        t_buf[j] = total.astype(jnp.bfloat16)
        for step in range(n_z - 1, 0, -1):
            push(
                t_buf.at[j, z_next(step)],
                r_z.at[j, step - 1],
                rz_send.at[j, step],
                rz_recv.at[j, step],
                peer(z_next(step), c, y),
            )

    def finish(j):
        total = t_buf[j, z].astype(jnp.float32)
        for step in range(1, n_z):
            arrived(
                r_z.at[j, step - 1],
                rz_send.at[j, step],
                rz_recv.at[j, step],
                peer(z_next(step), c, y),
            )
            total = total + r_z[j, step - 1].astype(jnp.float32)
        final[...] = total
        for q in range(QUARTERS):
            span = slice(q * width + j * chunk, q * width + (j + 1) * chunk)
            out[:, span] = final[q * rows : (q + 1) * rows, :].astype(out.dtype)

    for t in range(CHUNKS + 3 * LAG):
        for late, stage_of in enumerate((produce, over_y, over_z, finish)):
            if 0 <= t - late * LAG < CHUNKS:
                stage_of(t - late * LAG)
    for copy in sent:
        copy.wait_send()


def body(tokens, route_ids, route_weight, gate_weight, up_weight, down_weight):
    rows, features = tokens.shape
    n_z = lax.axis_size("expert") // CORES
    n_y = lax.axis_size("cuts")
    experts, _, units = gate_weight.shape
    width = features // QUARTERS
    chunk = width // CHUNKS
    plane = n_z * n_y
    blocks = CORES * plane
    groups = blocks // GROUP
    bf16, f32 = jnp.bfloat16, jnp.float32
    dma = pltpu.SemaphoreType.DMA
    vmem = pl.BlockSpec(memory_space=pltpu.VMEM)
    hbm = pl.BlockSpec(memory_space=pl.ANY)
    return pl.pallas_call(
        functools.partial(kernel, n_z, n_y),
        out_shape=jax.ShapeDtypeStruct((rows, features), bf16),
        in_specs=[vmem, vmem, vmem, hbm, hbm, hbm],
        out_specs=vmem,
        scratch_shapes=[
            pltpu.VMEM(gate_weight.shape, bf16),
            pltpu.VMEM(up_weight.shape, bf16),
            pltpu.VMEM(down_weight.shape, bf16),
            pltpu.VMEM((blocks, TILE, width + BLOCK), bf16),
            pltpu.VMEM((TILE, width + BLOCK), f32),
            pltpu.VMEM((groups, 2, experts, GROUP * rows, units), f32),
            pltpu.VMEM((groups, experts, GROUP * rows, units), bf16),
            pltpu.VMEM((groups, GROUP * TILE, width), bf16),
            pltpu.VMEM((CHUNKS, blocks, TILE, chunk), bf16),
            pltpu.VMEM((CHUNKS, plane, TILE, chunk), bf16),
            pltpu.VMEM((CHUNKS, n_y - 1, n_z, TILE, chunk), bf16),
            pltpu.VMEM((CHUNKS, n_y - 1, n_z, TILE, chunk), bf16),
            pltpu.VMEM((CHUNKS, n_z, TILE, chunk), bf16),
            pltpu.VMEM((CHUNKS, n_z - 1, TILE, chunk), bf16),
            pltpu.VMEM((TILE, chunk), f32),
            dma((2 * QUARTERS,)),
            dma((2 * QUARTERS,)),
            dma(down_weight.shape[:1]),
            dma((2, n_z)),
            dma((2, n_z)),
            dma((2, n_y, n_z)),
            dma((2, n_y, n_z)),
            dma((2, n_y, n_z)),
            dma((2, n_y, n_z)),
            dma((CHUNKS,)),
            dma((CHUNKS,)),
            dma((CHUNKS, n_y)),
            dma((CHUNKS, n_y)),
            dma((CHUNKS, n_z)),
            dma((CHUNKS, n_z)),
        ],
        compiler_params=pltpu.CompilerParams(
            collective_id=0, has_side_effects=True, vmem_limit_bytes=52 * 1024 * 1024
        ),
    )(tokens, route_ids, route_weight, gate_weight, up_weight, down_weight)


def solution(mesh):
    in_specs = (
        P(("parts", "expert", "cuts"), None),
        P(("parts", "expert", "cuts"), None),
        P(("parts", "expert", "cuts"), None),
        P("expert", None, "cuts"),
        P("expert", None, "cuts"),
        P("expert", "cuts", None),
    )
    out_specs = P(("parts", "expert", "cuts"), None)
    return jax.shard_map(body, mesh=mesh, in_specs=in_specs, out_specs=out_specs, check_vma=False)
```

```python
import functools
import math

import jax
import jax.numpy as jnp
from jax import lax
from jax.experimental import pallas as pl
from jax.experimental.pallas import tpu as pltpu
from jax.sharding import PartitionSpec as P

BLOCK = 128
eps = 1e-06
levels = 127.0
CORES = 2
QUARTERS = 4
TILE = 16
GROUP = 16
CHUNKS = 7
LAG = 3
MESH = pl.DeviceIdType.MESH


def hadamard():
    row_bits = lax.broadcasted_iota(jnp.int32, (BLOCK, BLOCK), 0)
    col_bits = lax.broadcasted_iota(jnp.int32, (BLOCK, BLOCK), 1)
    shared = jnp.bitwise_and(row_bits, col_bits)
    for shift in (4, 2, 1):
        shared = jnp.bitwise_xor(shared, jnp.right_shift(shared, shift))
    return (1 - 2 * jnp.bitwise_and(shared, 1)).astype(jnp.float32).astype(jnp.bfloat16)


def permutation(rows, transposed):
    side = GROUP * TILE
    a = lax.broadcasted_iota(jnp.int32, (side, side), 1 if transposed else 0)
    b = lax.broadcasted_iota(jnp.int32, (side, side), 0 if transposed else 1)
    per = GROUP * rows
    quarter, inner = a // per, a % per
    source = (inner // rows) * TILE + quarter * rows + inner % rows
    return jnp.where(source == b, 1.0, 0.0).astype(jnp.bfloat16)


def kernel(
    n_z,
    n_y,
    tokens,
    ids,
    weights,
    gate_hbm,
    up_hbm,
    down_hbm,
    out,
    gate,
    up,
    down,
    gathered,
    stage,
    acc,
    hid,
    wide,
    y_buf,
    r_core,
    s_buf,
    r_y,
    t_buf,
    r_z,
    final,
    g_sem,
    u_sem,
    d_sem,
    az_send,
    az_recv,
    ay_send,
    ay_recv,
    ac_send,
    ac_recv,
    rc_send,
    rc_recv,
    ry_send,
    ry_recv,
    rz_send,
    rz_recv,
):
    rows, features = tokens.shape
    experts = gate.shape[0]
    units = gate.shape[2]
    width = features // QUARTERS
    chunk = width // CHUNKS
    plane = n_y * n_z
    blocks = CORES * plane
    groups = blocks // GROUP
    expert = lax.axis_index("expert")
    y = lax.axis_index("cuts")
    z, c = expert // CORES, expert % CORES
    far = 1 - c
    cut = (width // 256 + 1) // 2 * 256
    spans = ((0, cut), (cut, width + BLOCK))

    def peer(z_at, c_at, y_at):
        return {"expert": z_at * CORES + c_at, "cuts": y_at}

    def block(c_at, y_at, z_at):
        return (c_at * n_y + y_at) * n_z + z_at

    def z_next(step):
        return lax.rem(z + step, n_z)

    def y_next(step):
        return lax.rem(y + step, n_y)

    def z_prev(step):
        return lax.rem(z + n_z - step, n_z)

    def y_prev(step):
        return lax.rem(y + n_y - step, n_y)

    gate_in, up_in, down_in = [], [], []
    for h in range(2):
        low, high = spans[h][0], min(spans[h][1], width)
        for q in range(QUARTERS):
            span = pl.ds(q * width + low, high - low)
            at = h * QUARTERS + q
            gate_in.append(
                pltpu.make_async_copy(gate_hbm.at[:, span, :], gate.at[:, span, :], g_sem.at[at])
            )
            up_in.append(
                pltpu.make_async_copy(up_hbm.at[:, span, :], up.at[:, span, :], u_sem.at[at])
            )
            gate_in[at].start()
            up_in[at].start()
    for e in range(experts):
        down_in.append(pltpu.make_async_copy(down_hbm.at[e], down.at[e], d_sem.at[e]))
        down_in[e].start()

    barrier = pltpu.get_barrier_semaphore()
    for step in range(1, n_z):
        pl.semaphore_signal(
            barrier, inc=1, device_id=peer(z_next(step), c, y), device_id_type=MESH
        )
    for step in range(1, n_y):
        pl.semaphore_signal(
            barrier, inc=1, device_id=peer(z, c, y_next(step)), device_id_type=MESH
        )
    pl.semaphore_signal(barrier, inc=1, device_id=peer(z, far, y), device_id_type=MESH)

    mine = block(c, y, z)
    for q in range(QUARTERS):
        stage[q * rows : (q + 1) * rows, :width] = tokens[:, q * width : (q + 1) * width].astype(
            jnp.float32
        )
    pieces = width // BLOCK
    stacked = jnp.concatenate(
        [stage[:, b * BLOCK : (b + 1) * BLOCK].astype(jnp.bfloat16) for b in range(pieces)], axis=0
    )
    rotated = jnp.dot(stacked, hadamard(), preferred_element_type=jnp.float32) * (
        1.0 / math.sqrt(BLOCK)
    )
    largest = jnp.max(jnp.abs(rotated), axis=1, keepdims=True) + eps
    quantized = jnp.clip(jnp.floor(rotated / largest * levels + 0.5), -levels, levels)
    restored = (quantized * largest / levels).astype(jnp.bfloat16)
    for b in range(pieces):
        gathered[mine, :, b * BLOCK : (b + 1) * BLOCK] = restored[b * TILE : (b + 1) * TILE, :]
    lane = lax.broadcasted_iota(jnp.int32, (rows, BLOCK), 1)
    dense = jnp.zeros((rows, BLOCK), jnp.float32)
    for k in range(ids.shape[1]):
        dense = dense + jnp.where(ids[:, k : k + 1] == lane, weights[:, k : k + 1], 0.0)
    stage[:, width:] = jnp.zeros((TILE, BLOCK), jnp.float32)
    for q in range(3):
        term = dense.astype(jnp.bfloat16).astype(jnp.float32)
        stage[q * rows : (q + 1) * rows, width:] = term
        dense = dense - term
    gathered[mine, :, width:] = stage[:, width:].astype(jnp.bfloat16)

    pl.semaphore_wait(barrier, n_z + n_y - 1)

    sent = []

    def push(src, dst, send_sem, recv_sem, device):
        copy = pltpu.make_async_remote_copy(
            src_ref=src,
            dst_ref=dst,
            send_sem=send_sem,
            recv_sem=recv_sem,
            device_id=device,
            device_id_type=MESH,
        )
        copy.start()
        sent.append(copy)

    def arrived(dst, send_sem, recv_sem, device):
        pltpu.make_async_remote_copy(
            src_ref=dst,
            dst_ref=dst,
            send_sem=send_sem,
            recv_sem=recv_sem,
            device_id=device,
            device_id_type=MESH,
        ).wait_recv()

    def half(h, slot):
        return gathered.at[slot, :, pl.ds(spans[h][0], spans[h][1] - spans[h][0])]

    def to_y(h, z_step, slot):
        for step in range(1, n_y):
            push(
                half(h, slot),
                half(h, slot),
                ay_send.at[h, step, z_step],
                ay_recv.at[h, step, z_step],
                peer(z, c, y_next(step)),
            )

    def to_core(h, y_step, z_step, slot):
        push(
            half(h, slot),
            half(h, slot),
            ac_send.at[h, y_step, z_step],
            ac_recv.at[h, y_step, z_step],
            peer(z, far, y),
        )

    def begin(h):
        for step in range(1, n_z):
            push(
                half(h, mine),
                half(h, mine),
                az_send.at[h, step],
                az_recv.at[h, step],
                peer(z_next(step), c, y),
            )
        to_y(h, 0, mine)
        to_core(h, 0, 0, mine)

    def from_z(h, z_step):
        slot = block(c, y, z_prev(z_step))
        arrived(
            half(h, slot),
            az_send.at[h, z_step],
            az_recv.at[h, z_step],
            peer(z_next(z_step), c, y),
        )
        to_y(h, z_step, slot)
        to_core(h, 0, z_step, slot)

    def from_y(h, z_step, y_step):
        slot = block(c, y_prev(y_step), z_prev(z_step))
        arrived(
            half(h, slot),
            ay_send.at[h, y_step, z_step],
            ay_recv.at[h, y_step, z_step],
            peer(z, c, y_next(y_step)),
        )
        to_core(h, y_step, z_step, slot)

    def events(h):
        steps = [functools.partial(from_z, h, z_step) for z_step in range(1, n_z)]
        return steps + [
            functools.partial(from_y, h, z_step, y_step)
            for z_step in range(n_z)
            for y_step in range(1, n_y)
        ]

    def from_core(h):
        for z_step in range(n_z):
            for y_step in range(n_y):
                slot = block(far, y_prev(y_step), z_prev(z_step))
                arrived(
                    half(h, slot),
                    ac_send.at[h, y_step, z_step],
                    ac_recv.at[h, y_step, z_step],
                    peer(z, far, y),
                )

    begin(0)
    begin(1)
    first, second = events(0), events(1)
    for event in first[: n_z - 1] + second[: n_z - 1] + first[n_z - 1 :]:
        event()
    pending = second[n_z - 1 :]
    each = -(-len(pending) // (2 * QUARTERS))

    order = permutation(rows, False)
    per = GROUP * rows
    route = []
    for h in range(2):
        for event in pending if h else []:
            event()
        from_core(h)
        low, high = spans[h][0], min(spans[h][1], width)
        for g in range(groups):
            flat = gathered[g * GROUP : (g + 1) * GROUP, :, low : spans[h][1]]
            flat = flat.reshape(GROUP * TILE, spans[h][1] - low)
            ordered = jnp.dot(order, flat, preferred_element_type=jnp.float32)
            wide[g, :, low:high] = ordered[:, : high - low].astype(jnp.bfloat16)
            if h:
                terms = ordered[:, high - low :]
                route.append(terms[:per] + terms[per : 2 * per] + terms[2 * per : 3 * per])
        for q in range(QUARTERS):
            span = slice(q * width + low, q * width + high)
            for side, (held, coming) in enumerate(((gate, gate_in), (up, up_in))):
                coming[h * QUARTERS + q].wait()
                for g in range(groups):
                    x = wide[g, q * per : (q + 1) * per, low:high]
                    for e in range(experts):
                        part = jnp.dot(x, held[e, span, :], preferred_element_type=jnp.float32)
                        acc[g, side, e] = part if h + q == 0 else acc[g, side, e] + part
                if h == 0:
                    for event in pending[:each]:
                        event()
                    pending = pending[each:]
    lanes = lax.broadcasted_iota(jnp.int32, (per, BLOCK), 1)
    scale = []
    for g in range(groups):
        for e in range(experts):
            v = acc[g, 0, e]
            hid[g, e] = (v / (1.0 + jnp.exp(-v)) * acc[g, 1, e]).astype(jnp.bfloat16)
            hit = lanes == expert * experts + e
            scale.append(jnp.sum(jnp.where(hit, route[g], 0.0), axis=1, keepdims=True))

    back = permutation(rows, True)
    for e in range(experts):
        down_in[e].wait()

    def produce(j):
        for g in range(groups):
            parts = []
            for q in range(QUARTERS):
                span = slice(q * width + j * chunk, q * width + (j + 1) * chunk)
                total = None
                for e in range(experts):
                    part = scale[g * experts + e] * jnp.dot(
                        hid[g, e], down[e, :, span], preferred_element_type=jnp.float32
                    )
                    total = part if total is None else total + part
                parts.append(total.astype(jnp.bfloat16))
            tiled = jnp.dot(
                back, jnp.concatenate(parts, axis=0), preferred_element_type=jnp.float32
            )
            y_buf[j, g * GROUP : (g + 1) * GROUP] = tiled.astype(jnp.bfloat16).reshape(
                GROUP, TILE, chunk
            )
        push(
            y_buf.at[j, pl.ds(far * plane, plane)],
            r_core.at[j],
            rc_send.at[j],
            rc_recv.at[j],
            peer(z, far, y),
        )

    def pair(j, y_at):
        own = y_buf[j, pl.ds(block(c, y_at, 0), n_z)].astype(jnp.float32)
        return own + r_core[j, pl.ds(y_at * n_z, n_z)].astype(jnp.float32)

    def over_y(j):
        arrived(r_core.at[j], rc_send.at[j], rc_recv.at[j], peer(z, far, y))
        for step in range(1, n_y):
            s_buf[j, step - 1] = pair(j, y_next(step)).astype(jnp.bfloat16)
            push(
                s_buf.at[j, step - 1],
                r_y.at[j, step - 1],
                ry_send.at[j, step],
                ry_recv.at[j, step],
                peer(z, c, y_next(step)),
            )

    def over_z(j):
        total = pair(j, y)
        for step in range(1, n_y):
            arrived(
                r_y.at[j, step - 1],
                ry_send.at[j, step],
                ry_recv.at[j, step],
                peer(z, c, y_next(step)),
            )
            total = total + r_y[j, step - 1].astype(jnp.float32)
        t_buf[j] = total.astype(jnp.bfloat16)
        for step in range(n_z - 1, 0, -1):
            push(
                t_buf.at[j, z_next(step)],
                r_z.at[j, step - 1],
                rz_send.at[j, step],
                rz_recv.at[j, step],
                peer(z_next(step), c, y),
            )

    def finish(j):
        total = t_buf[j, z].astype(jnp.float32)
        for step in range(1, n_z):
            arrived(
                r_z.at[j, step - 1],
                rz_send.at[j, step],
                rz_recv.at[j, step],
                peer(z_next(step), c, y),
            )
            total = total + r_z[j, step - 1].astype(jnp.float32)
        final[...] = total
        for q in range(QUARTERS):
            span = slice(q * width + j * chunk, q * width + (j + 1) * chunk)
            out[:, span] = final[q * rows : (q + 1) * rows, :].astype(out.dtype)

    for t in range(CHUNKS + 3 * LAG):
        for late, stage_of in reversed(tuple(enumerate((produce, over_y, over_z, finish)))):
            if 0 <= t - late * LAG < CHUNKS:
                stage_of(t - late * LAG)
    for copy in sent:
        copy.wait_send()


def body(tokens, route_ids, route_weight, gate_weight, up_weight, down_weight):
    rows, features = tokens.shape
    n_z = lax.axis_size("expert") // CORES
    n_y = lax.axis_size("cuts")
    experts, _, units = gate_weight.shape
    width = features // QUARTERS
    chunk = width // CHUNKS
    plane = n_z * n_y
    blocks = CORES * plane
    groups = blocks // GROUP
    bf16, f32 = jnp.bfloat16, jnp.float32
    dma = pltpu.SemaphoreType.DMA
    vmem = pl.BlockSpec(memory_space=pltpu.VMEM)
    hbm = pl.BlockSpec(memory_space=pl.ANY)
    return pl.pallas_call(
        functools.partial(kernel, n_z, n_y),
        out_shape=jax.ShapeDtypeStruct((rows, features), bf16),
        in_specs=[vmem, vmem, vmem, hbm, hbm, hbm],
        out_specs=vmem,
        scratch_shapes=[
            pltpu.VMEM(gate_weight.shape, bf16),
            pltpu.VMEM(up_weight.shape, bf16),
            pltpu.VMEM(down_weight.shape, bf16),
            pltpu.VMEM((blocks, TILE, width + BLOCK), bf16),
            pltpu.VMEM((TILE, width + BLOCK), f32),
            pltpu.VMEM((groups, 2, experts, GROUP * rows, units), f32),
            pltpu.VMEM((groups, experts, GROUP * rows, units), bf16),
            pltpu.VMEM((groups, GROUP * TILE, width), bf16),
            pltpu.VMEM((CHUNKS, blocks, TILE, chunk), bf16),
            pltpu.VMEM((CHUNKS, plane, TILE, chunk), bf16),
            pltpu.VMEM((CHUNKS, n_y - 1, n_z, TILE, chunk), bf16),
            pltpu.VMEM((CHUNKS, n_y - 1, n_z, TILE, chunk), bf16),
            pltpu.VMEM((CHUNKS, n_z, TILE, chunk), bf16),
            pltpu.VMEM((CHUNKS, n_z - 1, TILE, chunk), bf16),
            pltpu.VMEM((TILE, chunk), f32),
            dma((2 * QUARTERS,)),
            dma((2 * QUARTERS,)),
            dma(down_weight.shape[:1]),
            dma((2, n_z)),
            dma((2, n_z)),
            dma((2, n_y, n_z)),
            dma((2, n_y, n_z)),
            dma((2, n_y, n_z)),
            dma((2, n_y, n_z)),
            dma((CHUNKS,)),
            dma((CHUNKS,)),
            dma((CHUNKS, n_y)),
            dma((CHUNKS, n_y)),
            dma((CHUNKS, n_z)),
            dma((CHUNKS, n_z)),
        ],
        compiler_params=pltpu.CompilerParams(
            collective_id=0, has_side_effects=True, vmem_limit_bytes=52 * 1024 * 1024
        ),
    )(tokens, route_ids, route_weight, gate_weight, up_weight, down_weight)


def solution(mesh):
    in_specs = (
        P(("parts", "expert", "cuts"), None),
        P(("parts", "expert", "cuts"), None),
        P(("parts", "expert", "cuts"), None),
        P("expert", None, "cuts"),
        P("expert", None, "cuts"),
        P("expert", "cuts", None),
    )
    out_specs = P(("parts", "expert", "cuts"), None)
    return jax.shard_map(body, mesh=mesh, in_specs=in_specs, out_specs=out_specs, check_vma=False)
```
